256 devices in a mesh: section: 32 (over z, y_lo, core), dp: 8 (over x, y_hi).
Axes of the slice: x: 4, y: 4 (y_hi: 2, y_lo: 2; y = y_hi * 2 + y_lo), z: 8, core: 2. Of those that a mesh axis runs over, the one named last changes fastest.
Arguments:
- inputs: bfloat16 [1024, 2560], P('dp'), may hold values from -6 to 6
- cotangent: bfloat16 [1024, 2560], P('dp'), may hold values from -6 to 6
- weights: bfloat16 [32, 2560, 2560], P('section', 'dp'), may hold values from -0.125 to 0.125
- adam_m: float32 [32, 2560, 2560], P('section', 'dp'), may hold values from -0.0064 to 0.0064
- adam_v: float32 [32, 2560, 2560], P('section', 'dp'), may hold values from 5e-06 to 6e-05
Outputs:
- update: bfloat16 [32, 2560, 2560], P('section', 'dp')
- shadow_weights: bfloat16 [32, 2560, 2560], P('section', 'dp')
- shadow_acts: bfloat16 [32, 1024, 2560], P('section', 'dp')
The draws below stay inside these ranges and needn't reach their ends.
All inputs are finite; a program needn't handle non-finite values.
Results may differ from the reference program's by a relative error of at most 0.03.
Values may be sent and summed in bfloat16 or wider, within the bound.
A program may use at most 128 MiB of HBM per device.

```python
import math
import jax
import jax.numpy as jnp
from jax import lax

D = 2560
TOKENS = 1024
LAYERS = 32


def block_scale(own_key, dims, split, least, largest):
    factor_of = 1.0
    for dim, blocks in split:
        draws = jax.random.uniform(jax.random.fold_in(jax.random.fold_in(own_key, 6), dim), (blocks,), jnp.float32, least / len(split), largest / len(split))
        factor_of = factor_of * jnp.repeat(jnp.exp(draws), dims[dim] // blocks).reshape((-1,) + (1,) * (len(dims) - 1 - dim))
    return factor_of


def bell_draw(own_key, dims, deviation, limit, pieces=(), held_as=jnp.bfloat16):
    values = deviation * jax.random.normal(own_key, dims, jnp.float32)
    if pieces:
        values = values * block_scale(own_key, dims, pieces, -0.22, 0.18)
    return jnp.clip(values, -limit, limit).astype(held_as)


def setup_inputs(seed: int = 0) -> dict:
    keys = jax.random.split(jax.random.key(seed), 6)
    return {
        "inputs": bell_draw(keys[0], (TOKENS, D), 1.0, 6.0, ((0, 8),)),
        "cotangent": bell_draw(keys[1], (TOKENS, D), 1.0, 6.0, ((0, 8),)),
        "weights": bell_draw(keys[2], (LAYERS, D, D), D ** -0.5, 0.125, ((0, 32), (1, 8))),
        "adam_m": bell_draw(keys[3], (LAYERS, D, D), 0.0016, 0.0064, ((0, 32), (1, 8)), jnp.float32),
        "adam_v": jnp.clip(jnp.exp(math.log(5.999999848427251e-05) - 2.4849066 * jax.random.uniform(keys[4], (LAYERS, D, D), jnp.float32) ** block_scale(keys[4], (LAYERS, D, D), ((0, 32), (1, 8)), -0.2, 0.2)), 4.999999873689376e-06, 5.999999848427251e-05),
    }


branch_scale = 0.5
norm_eps = 1e-05
beta_one = 0.9
beta_two = 0.95
adam_eps = 1e-08
learn_rate = 0.01
step_count = 4.0
tanh_coef = 0.7978845608028654
cubic_coef = 0.044715

def gelu_value(values):
    tanh_part = jnp.tanh(tanh_coef * (values + cubic_coef * values * values * values))
    return 0.5 * values * (1.0 + tanh_part)

def gelu_slope(values):
    tanh_part = jnp.tanh(tanh_coef * (values + cubic_coef * values * values * values))
    return 0.5 * (1.0 + tanh_part) + 0.5 * values * (1.0 - tanh_part * tanh_part) * tanh_coef * (1.0 + 3.0 * cubic_coef * values * values)

def normalize(current):
    as_float = current.astype(jnp.float32)
    inv_rms = lax.rsqrt(lax.optimization_barrier(jnp.mean(as_float * as_float, axis=-1, keepdims=True)) + norm_eps)
    return (as_float, inv_rms, as_float * inv_rms)

def adam_step(weight, moment_one, moment_two, gradient):
    moment_one = beta_one * moment_one + (1.0 - beta_one) * gradient
    moment_two = beta_two * moment_two + (1.0 - beta_two) * gradient * gradient
    corrected_one = moment_one / (1.0 - beta_one ** step_count)
    corrected_two = moment_two / (1.0 - beta_two ** step_count)
    direction = corrected_one / (jnp.sqrt(corrected_two) + adam_eps)
    new_weight = (weight.astype(jnp.float32) - learn_rate * direction).astype(jnp.bfloat16)
    return (direction.astype(jnp.bfloat16), new_weight)

def reference(inputs, cotangent, weights, adam_m, adam_v):
    token_count = inputs.shape[0]

    def forward_layer(current, weight):
        as_float, inv_rms, normed = normalize(current)
        pre_act = jnp.dot(normed.astype(jnp.bfloat16), weight, preferred_element_type=jnp.float32)
        output = (as_float + branch_scale * gelu_value(pre_act)).astype(jnp.bfloat16)
        return (output, (current, output))
    unused, (layer_inputs, layer_outputs) = lax.scan(forward_layer, inputs, weights)

    def backward_layer(grad_out, layer_data):
        current, weight, moment_one, moment_two = layer_data
        as_float, inv_rms, normed = normalize(current)
        normed_low = normed.astype(jnp.bfloat16)
        pre_act = jnp.dot(normed_low, weight, preferred_element_type=jnp.float32)
        grad_float = grad_out.astype(jnp.float32)
        grad_pre = (grad_float * branch_scale * gelu_slope(pre_act)).astype(jnp.bfloat16)
        grad_normed = jnp.dot(grad_pre, weight.T, preferred_element_type=jnp.float32)
        grad_in = grad_float + inv_rms * (grad_normed - normed * lax.optimization_barrier(jnp.mean(grad_normed * normed, axis=-1, keepdims=True)))
        gradient = jnp.dot(normed_low.T, grad_pre, preferred_element_type=jnp.float32) / token_count
        direction, new_weight = adam_step(weight, moment_one, moment_two, gradient)
        return (grad_in.astype(jnp.bfloat16), (direction, new_weight))
    unused_grad, (update, new_weights) = lax.scan(backward_layer, cotangent, (layer_inputs, weights, adam_m, adam_v), reverse=True)
    return (update, jnp.roll(new_weights, -1, axis=0), jnp.roll(layer_outputs, -1, axis=0))
```

```python
import functools
import jax
import jax.numpy as jnp
from jax import lax
from jax.experimental import pallas as pl
from jax.experimental.pallas import tpu as pltpu
from jax.sharding import PartitionSpec as P

MICRO = 8
CHUNK = 256

branch_scale = 0.5
norm_eps = 1e-05
beta_one = 0.9
beta_two = 0.95
adam_eps = 1e-08
learn_rate = 0.01
step_count = 4.0
tanh_coef = 0.7978845608028654
cubic_coef = 0.044715


def adam_step(weight, moment_one, moment_two, gradient):
    moment_one = beta_one * moment_one + (1.0 - beta_one) * gradient
    moment_two = beta_two * moment_two + (1.0 - beta_two) * gradient * gradient
    corrected_one = moment_one / (1.0 - beta_one**step_count)
    corrected_two = moment_two / (1.0 - beta_two**step_count)
    direction = corrected_one / (jnp.sqrt(corrected_two) + adam_eps)
    new_weight = (weight.astype(jnp.float32) - learn_rate * direction).astype(jnp.bfloat16)
    return (direction.astype(jnp.bfloat16), new_weight)


def chain_kernel(
    sections,
    inputs_ref,
    cotangent_ref,
    weight_ref,
    normed_ref,
    grads_ref,
    shadow_ref,
    weight,
    flipped,
    arrived,
    outputs,
    grads_in,
    grads_out,
    pre_acts,
    slopes,
    scales,
    load_sem,
    ahead_send,
    ahead_recv,
    back_send,
    back_recv,
    shadow_send,
    shadow_recv,
):
    micro, rows, width = arrived.shape
    me = lax.axis_index("section")
    after = lax.rem(me + 1, sections)
    before = lax.rem(me + sections - 1, sections)

    load = pltpu.make_async_copy(weight_ref, weight, load_sem)
    load.start()
    barrier = pltpu.get_barrier_semaphore()
    for peer in (before, after):
        pl.semaphore_signal(barrier, inc=1, device_id={"section": peer})
    pl.semaphore_wait(barrier, 2)

    def ahead(i):
        return pltpu.make_async_remote_copy(
            src_ref=outputs.at[i],
            dst_ref=arrived.at[i],
            send_sem=ahead_send.at[i],
            recv_sem=ahead_recv.at[i],
            device_id={"section": after},
        )

    def back(i):
        return pltpu.make_async_remote_copy(
            src_ref=grads_out.at[i],
            dst_ref=grads_in.at[i],
            send_sem=back_send.at[i],
            recv_sem=back_recv.at[i],
            device_id={"section": before},
        )

    def shadow(i):
        return pltpu.make_async_remote_copy(
            src_ref=outputs.at[i],
            dst_ref=shadow_ref.at[i],
            send_sem=shadow_send.at[i],
            recv_sem=shadow_recv.at[i],
            device_id={"section": before},
        )

    def flip():
        blocks = width // CHUNK

        def one(k, carry):
            row = pl.multiple_of((k // blocks) * CHUNK, CHUNK)
            column = pl.multiple_of(lax.rem(k, blocks) * CHUNK, CHUNK)
            flipped[pl.ds(column, CHUNK), pl.ds(row, CHUNK)] = weight[
                pl.ds(row, CHUNK), pl.ds(column, CHUNK)
            ].T
            return carry

        lax.fori_loop(0, blocks * blocks, one, 0)

    load.wait()

    @pl.when(me == 0)
    def _():
        arrived[...] = inputs_ref[...]

    @pl.when(me == sections - 1)
    def _():
        grads_in[...] = cotangent_ref[...]

    @pl.when(me >= sections // 2)
    def _():
        flip()

    def forward(i, carry):
        @pl.when(me > 0)
        def _():
            ahead(i).wait_recv()

        current = arrived[i].astype(jnp.float32)
        scale = lax.rsqrt(jnp.mean(current * current, axis=-1, keepdims=True) + norm_eps)
        scales[i] = jnp.broadcast_to(scale, (rows, 128))
        normed = (current * scale).astype(jnp.bfloat16)
        normed_ref[i] = normed
        for at in range(0, width, CHUNK):
            part = pl.ds(at, CHUNK)
            v = jnp.dot(normed, weight[:, part], preferred_element_type=jnp.float32)
            t = jnp.tanh(tanh_coef * (v + cubic_coef * v * v * v))
            out = arrived[i, :, part].astype(jnp.float32) + branch_scale * (0.5 * v * (1.0 + t))
            outputs[i, :, part] = out.astype(jnp.bfloat16)
            pre_acts[i, :, part] = v
            slope = 0.5 * (1.0 + t) + 0.5 * v * (1.0 - t * t) * tanh_coef * (
                1.0 + 3.0 * cubic_coef * v * v
            )
            slopes[i, :, part] = branch_scale * slope

        @pl.when(me < sections - 1)
        def _():
            ahead(i).start()

        shadow(i).start()
        return carry

    lax.fori_loop(0, micro, forward, 0)

    @pl.when(me < sections // 2)
    def _():
        flip()

    def backward(i, carry):
        @pl.when(me < sections - 1)
        def _():
            back(i).wait_recv()

        grad = grads_in[i].astype(jnp.float32)
        grad_pre = (grad * slopes[i]).astype(jnp.bfloat16)
        grads_ref[i] = grad_pre

        @pl.when(me > 0)
        def _():
            overlap = jnp.sum(
                grad_pre.astype(jnp.float32) * pre_acts[i], axis=-1, keepdims=True
            ) * (1.0 / width)
            scale = scales[i][:, :1]
            pull = scale * scale * overlap
            for at in range(0, width, CHUNK):
                part = pl.ds(at, CHUNK)
                g = jnp.dot(grad_pre, flipped[:, part], preferred_element_type=jnp.float32)
                a = arrived[i, :, part].astype(jnp.float32)
                total = grads_in[i, :, part].astype(jnp.float32) + scale * g - pull * a
                grads_out[i, :, part] = total.astype(jnp.bfloat16)
            back(i).start()

        return carry

    lax.fori_loop(0, micro, backward, 0)

    def settle(i, carry):
        @pl.when(me < sections - 1)
        def _():
            ahead(i).wait_send()

        @pl.when(me > 0)
        def _():
            back(i).wait_send()

        shadow(i).wait_send()
        shadow(i).wait_recv()
        return carry

    lax.fori_loop(0, micro, settle, 0)


def chain(sections, inputs, cotangent, full_weight):
    tokens, width = inputs.shape
    rows = tokens // MICRO
    block = (MICRO, rows, width)
    low = jax.ShapeDtypeStruct(block, jnp.bfloat16)
    in_vmem = pl.BlockSpec(memory_space=pltpu.VMEM)
    anywhere = pl.BlockSpec(memory_space=pl.ANY)
    return pl.pallas_call(
        functools.partial(chain_kernel, sections),
        out_shape=(low, low, low),
        in_specs=[in_vmem, in_vmem, anywhere],
        out_specs=(in_vmem, in_vmem, anywhere),
        scratch_shapes=[
            pltpu.VMEM((width, width), jnp.bfloat16),
            pltpu.VMEM((width, width), jnp.bfloat16),
            pltpu.VMEM(block, jnp.bfloat16),
            pltpu.VMEM(block, jnp.bfloat16),
            pltpu.VMEM(block, jnp.bfloat16),
            pltpu.VMEM(block, jnp.bfloat16),
            pltpu.VMEM(block, jnp.float32),
            pltpu.VMEM(block, jnp.float32),
            pltpu.VMEM((MICRO, rows, 128), jnp.float32),
            pltpu.SemaphoreType.DMA,
        ]
        + [pltpu.SemaphoreType.DMA((MICRO,))] * 6,
        compiler_params=pltpu.CompilerParams(
            collective_id=0, has_side_effects=True, vmem_limit_bytes=56 * 2**20
        ),
        cost_estimate=pl.CostEstimate(
            flops=4 * tokens * width * width,
            bytes_accessed=2 * width * width,
            transcendentals=tokens * width,
        ),
    )(inputs.reshape(block), cotangent.reshape(block), full_weight)


def on_device(inputs, cotangent, weights, adam_m, adam_v):
    sections = lax.axis_size("section")
    tokens, width = inputs.shape
    full_weight = lax.all_gather(weights[0], "dp", axis=0, tiled=True)
    normed, grads, shadow_output = chain(sections, inputs, cotangent, full_weight)
    normed = normed.reshape(tokens, width)
    grads = grads.reshape(tokens, width)
    unit_rows = lax.all_to_all(normed, "dp", split_axis=1, concat_axis=0, tiled=True)
    gathered = lax.all_gather(grads, "dp", axis=0, tiled=True)
    gradient = (
        lax.dot_general(
            unit_rows, gathered, (((0,), (0,)), ((), ())), preferred_element_type=jnp.float32
        )
        / gathered.shape[0]
    )
    direction, new_weight = adam_step(weights[0], adam_m[0], adam_v[0], gradient)
    shift = [(i, (i - 1) % sections) for i in range(sections)]
    shadow_weight = lax.ppermute(new_weight, "section", shift)
    return (direction[None], shadow_weight[None], shadow_output.reshape(1, tokens, width))


def solution(mesh):
    in_specs = (
        P("dp", None),
        P("dp", None),
        P("section", "dp", None),
        P("section", "dp", None),
        P("section", "dp", None),
    )
    out_specs = (P("section", "dp", None), P("section", "dp", None), P("section", "dp", None))
    return jax.shard_map(
        on_device, mesh=mesh, in_specs=in_specs, out_specs=out_specs, check_vma=False
    )
```

```python
import functools
import jax
import jax.numpy as jnp
from jax import lax
from jax.experimental import pallas as pl
from jax.experimental.pallas import tpu as pltpu
from jax.sharding import PartitionSpec as P

MICRO = 8
CHUNK = 256
PIECES = 4
WINDOW = 384

branch_scale = 0.5
norm_eps = 1e-05
beta_one = 0.9
beta_two = 0.95
adam_eps = 1e-08
learn_rate = 0.01
step_count = 4.0
tanh_coef = 0.7978845608028654
cubic_coef = 0.044715


def chain_kernel(
    sections,
    replicas,
    inputs_ref,
    cotangent_ref,
    shard_ref,
    moment_one_ref,
    moment_two_ref,
    update_ref,
    shadow_weight_ref,
    shadow_ref,
    weight,
    flipped,
    arrived,
    outputs,
    grads_in,
    grads_out,
    pre_acts,
    slopes,
    scales,
    normed_all,
    units,
    units_flipped,
    gathered,
    moment_one,
    moment_two,
    fresh,
    stage,
    load_sem,
    ahead_send,
    ahead_recv,
    back_send,
    back_recv,
    shadow_send,
    shadow_recv,
    weight_send,
    weight_recv,
    grad_send,
    grad_recv,
    unit_send,
    unit_recv,
    fresh_send,
    fresh_recv,
):
    micro, rows, width = arrived.shape
    shard = width // replicas
    piece = shard // PIECES
    ring = replicas // 2
    tokens = micro * rows
    blocks = width // CHUNK
    me = lax.axis_index("section")
    mine = lax.axis_index("dp")
    after = lax.rem(me + 1, sections)
    before = lax.rem(me + sections - 1, sections)
    line, side = mine // 2, lax.rem(mine, 2)

    def peer(step, across=False):
        return lax.rem(line + step + ring, ring) * 2 + (1 - side if across else side)

    right, left, facing, far = peer(1), peer(-1), peer(0, True), peer(2)

    loads = [
        pltpu.make_async_copy(
            shard_ref,
            weight.at[pl.ds(pl.multiple_of(mine * shard, 16), shard)],
            load_sem.at[0],
        ),
        pltpu.make_async_copy(moment_one_ref, moment_one, load_sem.at[1]),
        pltpu.make_async_copy(moment_two_ref, moment_two, load_sem.at[2]),
    ]
    loads[0].start()
    barrier = pltpu.get_barrier_semaphore()
    for other in (before, after):
        pl.semaphore_signal(barrier, inc=1, device_id={"section": other})
    for step in range(1, replicas):
        pl.semaphore_signal(barrier, inc=1, device_id={"dp": lax.rem(mine + step, replicas)})
    pl.semaphore_wait(barrier, replicas + 1)

    def spread_over(place, own, sends, recvs):
        def move(lane, owner, i, to, source=None):
            return pltpu.make_async_remote_copy(
                src_ref=place(owner, i) if source is None else source,
                dst_ref=place(owner, i),
                send_sem=sends.at[lane, i],
                recv_sem=recvs.at[owner, i],
                device_id={"dp": to},
            )

        def landed(owner, i):
            move(0, owner, i, mine).wait_recv()

        def spread(i):
            for lane, to in enumerate((facing, right, left)):
                move(lane, mine, i, to, own(i)).start()

        def relay(i):
            turn = 2 * lax.rem(i, 2) - 1
            landed(peer(turn), i)
            move(3, peer(turn), i, peer(-turn)).start()
            landed(facing, i)
            move(4, facing, i, right).start()
            move(5, facing, i, left).start()

        def cross(i):
            landed(far, i)
            move(6, far, i, facing).start()

        def finish(i):
            turn = 2 * lax.rem(i, 2) - 1
            landed(peer(-turn), i)
            landed(peer(1, True), i)
            landed(peer(-1, True), i)
            landed(peer(2, True), i)
            for lane in range(7):
                move(lane, mine, i, mine).wait_send()

        return spread, relay, cross, finish

    def each(count, *steps):
        for step in steps:

            def one(i, carry, step=step):
                step(i)
                return carry

            lax.fori_loop(0, count, one, 0)

    def weight_place(owner, i):
        return weight.at[pl.ds(pl.multiple_of(owner * shard + i * piece, 16), piece)]

    weight_spread = spread_over(
        weight_place,
        lambda i: shard_ref.at[pl.ds(pl.multiple_of(i * piece, 16), piece)],
        weight_send,
        weight_recv,
    )
    grad_spread, grad_relay, grad_cross, grad_finish = spread_over(
        lambda owner, i: gathered.at[owner, i],
        lambda i: gathered.at[mine, i],
        grad_send,
        grad_recv,
    )

    def ahead(i):
        return pltpu.make_async_remote_copy(
            src_ref=outputs.at[i],
            dst_ref=arrived.at[i],
            send_sem=ahead_send.at[i],
            recv_sem=ahead_recv.at[i],
            device_id={"section": after},
        )

    def back(i):
        return pltpu.make_async_remote_copy(
            src_ref=grads_out.at[i],
            dst_ref=grads_in.at[i],
            send_sem=back_send.at[i],
            recv_sem=back_recv.at[i],
            device_id={"section": before},
        )

    def shadow(i):
        return pltpu.make_async_remote_copy(
            src_ref=outputs.at[i],
            dst_ref=shadow_ref.at[i],
            send_sem=shadow_send.at[i],
            recv_sem=shadow_recv.at[i],
            device_id={"section": before},
        )

    def window(owner):
        start = (owner // 2) * (2 * shard) + lax.rem(owner, 2) * (2 * shard - WINDOW)
        return normed_all.at[:, :, pl.ds(pl.multiple_of(start, 128), WINDOW)]

    def unit(step):
        to = lax.rem(mine + step, replicas)
        return pltpu.make_async_remote_copy(
            src_ref=window(to),
            dst_ref=units.at[mine],
            send_sem=unit_send.at[step],
            recv_sem=unit_recv.at[step],
            device_id={"dp": to},
        )

    def columns(k):
        return pl.ds(pl.multiple_of(k * CHUNK, CHUNK), CHUNK)

    def fresh_move(k):
        return pltpu.make_async_remote_copy(
            src_ref=fresh.at[:, columns(k)],
            dst_ref=shadow_weight_ref.at[:, columns(k)],
            send_sem=fresh_send.at[k],
            recv_sem=fresh_recv.at[k],
            device_id={"section": before},
        )

    def flip(k):
        row, column = columns(k // blocks), columns(lax.rem(k, blocks))
        flipped[column, row] = weight[row, column].T

    each(PIECES, *weight_spread)
    loads[0].wait()
    loads[1].start()
    loads[2].start()

    @pl.when(me == 0)
    def _():
        arrived[...] = inputs_ref[...]

    @pl.when(me == sections - 1)
    def _():
        grads_in[...] = cotangent_ref[...]

    @pl.when(me >= sections // 2)
    def _():
        each(blocks * blocks, flip)

    def forward(i):
        @pl.when(me > 0)
        def _():
            ahead(i).wait_recv()

        current = arrived[i].astype(jnp.float32)
        scale = lax.rsqrt(jnp.mean(current * current, axis=-1, keepdims=True) + norm_eps)
        scales[i] = jnp.broadcast_to(scale, (rows, 128))
        normed = (current * scale).astype(jnp.bfloat16)
        normed_all[i] = normed
        for at in range(0, width, CHUNK):
            part = pl.ds(at, CHUNK)
            v = jnp.dot(normed, weight[:, part], preferred_element_type=jnp.float32)
            t = jnp.tanh(tanh_coef * (v + cubic_coef * v * v * v))
            out = arrived[i, :, part].astype(jnp.float32) + branch_scale * (0.5 * v * (1.0 + t))
            outputs[i, :, part] = out.astype(jnp.bfloat16)
            pre_acts[i, :, part] = v
            slope = 0.5 * (1.0 + t) + 0.5 * v * (1.0 - t * t) * tanh_coef * (
                1.0 + 3.0 * cubic_coef * v * v
            )
            slopes[i, :, part] = branch_scale * slope

        @pl.when(me < sections - 1)
        def _():
            ahead(i).start()

        shadow(i).start()

    each(micro, forward)

    def send_units():
        for step in range(1, replicas):
            unit(step).start()
        units[mine] = window(mine)[...]

    def flip_units():
        for step in range(1, replicas):
            unit(step).wait_recv()

        def one(k):
            block = units[k].reshape(tokens, WINDOW)
            units_flipped[:, pl.ds(pl.multiple_of(k * tokens, tokens), tokens)] = block.T

        each(replicas, one)

    @pl.when(me < sections // 2)
    def _():
        each(blocks * blocks, flip)
        send_units()
        flip_units()

    def backward(i):
        @pl.when(me < sections - 1)
        def _():
            back(i).wait_recv()

        grad = grads_in[i].astype(jnp.float32)
        grad_pre = (grad * slopes[i]).astype(jnp.bfloat16)
        gathered[mine, i] = grad_pre

        @pl.when(me > 0)
        def _():
            overlap = jnp.sum(
                grad_pre.astype(jnp.float32) * pre_acts[i], axis=-1, keepdims=True
            ) * (1.0 / width)
            scale = scales[i][:, :1]
            pull = scale * scale * overlap
            for at in range(0, width, CHUNK):
                part = pl.ds(at, CHUNK)
                g = jnp.dot(grad_pre, flipped[:, part], preferred_element_type=jnp.float32)
                a = arrived[i, :, part].astype(jnp.float32)
                total = grads_in[i, :, part].astype(jnp.float32) + scale * g - pull * a
                grads_out[i, :, part] = total.astype(jnp.bfloat16)
            back(i).start()

        grad_spread(i)

        @pl.when((me == 0) & (i > 0))
        def _():
            grad_relay(i - 1)

    each(micro, backward)

    @pl.when(me == 0)
    def _():
        grad_relay(micro - 1)

    @pl.when(me > 0)
    def _():
        each(micro, grad_relay)

    each(micro, grad_cross, grad_finish)

    @pl.when(me >= sections // 2)
    def _():
        send_units()
        flip_units()

    loads[1].wait()
    loads[2].wait()
    skip = lax.rem(mine, 2) * (WINDOW - shard)
    own_rows = mine * shard
    strip = shard // 5

    def step_weights(k):
        part = columns(k)
        grads = gathered[:, :, :, part].reshape(replicas * tokens, CHUNK)
        stage[...] = jnp.dot(units_flipped[...], grads, preferred_element_type=jnp.float32) * (
            1.0 / (replicas * tokens)
        )

        def adam(j):
            here = pl.ds(pl.multiple_of(j * strip, strip), strip)
            gradient = stage[pl.ds(pl.multiple_of(skip + j * strip, 16), strip), :]
            one = beta_one * moment_one[here, part] + (1.0 - beta_one) * gradient
            two = beta_two * moment_two[here, part] + (1.0 - beta_two) * gradient * gradient
            corrected_one = one * (1.0 / (1.0 - beta_one**step_count))
            corrected_two = two * (1.0 / (1.0 - beta_two**step_count))
            direction = corrected_one / (jnp.sqrt(corrected_two) + adam_eps)
            old = weight[pl.ds(pl.multiple_of(own_rows + j * strip, 16), strip), part]
            update_ref[here, part] = direction.astype(jnp.bfloat16)
            fresh[here, part] = (old.astype(jnp.float32) - learn_rate * direction).astype(
                jnp.bfloat16
            )

        each(5, adam)
        fresh_move(k).start()

    each(blocks, step_weights)

    def settle(i):
        @pl.when(me < sections - 1)
        def _():
            ahead(i).wait_send()

        @pl.when(me > 0)
        def _():
            back(i).wait_send()

        shadow(i).wait_send()
        shadow(i).wait_recv()

    def settle_fresh(k):
        fresh_move(k).wait_send()
        fresh_move(k).wait_recv()

    each(micro, settle)
    for step in range(1, replicas):
        unit(step).wait_send()
    each(blocks, settle_fresh)


def on_device(inputs, cotangent, weights, adam_m, adam_v):
    sections = lax.axis_size("section")
    replicas = lax.axis_size("dp")
    tokens, width = inputs.shape
    shard = width // replicas
    rows = tokens // MICRO
    block = (MICRO, rows, width)
    low = jnp.bfloat16
    wide = jnp.float32
    in_vmem = pl.BlockSpec(memory_space=pltpu.VMEM)
    anywhere = pl.BlockSpec(memory_space=pl.ANY)
    dma = pltpu.SemaphoreType.DMA
    update, shadow_weight, shadow_output = pl.pallas_call(
        functools.partial(chain_kernel, sections, replicas),
        out_shape=(
            jax.ShapeDtypeStruct((shard, width), low),
            jax.ShapeDtypeStruct((shard, width), low),
            jax.ShapeDtypeStruct(block, low),
        ),
        in_specs=[in_vmem, in_vmem, anywhere, anywhere, anywhere],
        out_specs=(in_vmem, anywhere, anywhere),
        scratch_shapes=[
            pltpu.VMEM((width, width), low),
            pltpu.VMEM((width, width), low),
            pltpu.VMEM(block, low),
            pltpu.VMEM(block, low),
            pltpu.VMEM(block, low),
            pltpu.VMEM(block, low),
            pltpu.VMEM(block, wide),
            pltpu.VMEM(block, wide),
            pltpu.VMEM((MICRO, rows, 128), wide),
            pltpu.VMEM(block, low),
            pltpu.VMEM((replicas, MICRO, rows, WINDOW), low),
            pltpu.VMEM((WINDOW, replicas * tokens), low),
            pltpu.VMEM((replicas,) + block, low),
            pltpu.VMEM((shard, width), wide),
            pltpu.VMEM((shard, width), wide),
            pltpu.VMEM((shard, width), low),
            pltpu.VMEM((WINDOW, CHUNK), wide),
            dma((3,)),
        ]
        + [dma((MICRO,))] * 6
        + [
            dma((7, PIECES)),
            dma((replicas, PIECES)),
            dma((7, MICRO)),
            dma((replicas, MICRO)),
            dma((replicas,)),
            dma((replicas,)),
            dma((width // CHUNK,)),
            dma((width // CHUNK,)),
        ],
        compiler_params=pltpu.CompilerParams(
            collective_id=0, has_side_effects=True, vmem_limit_bytes=60 * 2**20
        ),
        cost_estimate=pl.CostEstimate(
            flops=6 * tokens * width * width,
            bytes_accessed=16 * shard * width,
            transcendentals=tokens * width,
        ),
    )(
        inputs.reshape(block),
        cotangent.reshape(block),
        weights[0],
        adam_m[0],
        adam_v[0],
    )
    return (update[None], shadow_weight[None], shadow_output.reshape(1, tokens, width))


def solution(mesh):
    in_specs = (
        P("dp", None),
        P("dp", None),
        P("section", "dp", None),
        P("section", "dp", None),
        P("section", "dp", None),
    )
    out_specs = (P("section", "dp", None), P("section", "dp", None), P("section", "dp", None))
    return jax.shard_map(
        on_device, mesh=mesh, in_specs=in_specs, out_specs=out_specs, check_vma=False
    )
```

```python
import functools
import jax
import jax.numpy as jnp
from jax import lax
from jax.experimental import pallas as pl
from jax.experimental.pallas import tpu as pltpu
from jax.sharding import PartitionSpec as P

MICRO = 8
CHUNK = 256
PART = 512
APART = 2
PIECES = 4
WINDOW = 384

branch_scale = 0.5
norm_eps = 1e-05
beta_one = 0.9
beta_two = 0.95
adam_eps = 1e-08
learn_rate = 0.01
step_count = 4.0
tanh_coef = 0.7978845608028654
cubic_coef = 0.044715


def chain_kernel(
    sections,
    replicas,
    inputs_ref,
    cotangent_ref,
    shard_ref,
    moment_one_ref,
    moment_two_ref,
    update_ref,
    shadow_weight_ref,
    shadow_ref,
    weight,
    flipped,
    arrived,
    outputs,
    grads_in,
    grads_out,
    pre_acts,
    slopes,
    scales,
    normed_all,
    units,
    units_flipped,
    gathered,
    moment_one,
    moment_two,
    fresh,
    stage,
    sums,
    load_sem,
    ahead_send,
    ahead_recv,
    back_send,
    back_recv,
    shadow_send,
    shadow_recv,
    weight_send,
    weight_recv,
    grad_send,
    grad_recv,
    unit_send,
    unit_recv,
    fresh_send,
    fresh_recv,
    part_send,
    part_recv,
    passed,
):
    micro, rows, width = arrived.shape
    shard = width // replicas
    piece = shard // PIECES
    ring = replicas // 2
    tokens = micro * rows
    blocks = width // CHUNK
    pairs = micro // 2
    me = lax.axis_index("section")
    mine = lax.axis_index("dp")
    after = lax.rem(me + 1, sections)
    before = lax.rem(me + sections - 1, sections)
    line, side = mine // 2, lax.rem(mine, 2)

    def peer(step, across=False):
        return lax.rem(line + step + ring, ring) * 2 + (1 - side if across else side)

    right, left, facing, far = peer(1), peer(-1), peer(0, True), peer(2)

    loads = [
        pltpu.make_async_copy(
            shard_ref,
            weight.at[pl.ds(pl.multiple_of(mine * shard, 16), shard)],
            load_sem.at[0],
        ),
        pltpu.make_async_copy(moment_one_ref, moment_one, load_sem.at[1]),
        pltpu.make_async_copy(moment_two_ref, moment_two, load_sem.at[2]),
    ]
    loads[0].start()
    barrier = pltpu.get_barrier_semaphore()
    later = lax.rem(me + APART, sections)
    earlier = lax.rem(me + sections - APART, sections)
    for other in (before, after, earlier, later):
        pl.semaphore_signal(barrier, inc=1, device_id={"section": other})
    for step in range(1, replicas):
        pl.semaphore_signal(barrier, inc=1, device_id={"dp": lax.rem(mine + step, replicas)})
    pl.semaphore_wait(barrier, replicas + 3)

    def spread_over(place, own, sends, recvs, crosses):
        def move(lane, owner, i, to, source=None):
            return pltpu.make_async_remote_copy(
                src_ref=place(owner, i) if source is None else source,
                dst_ref=place(owner, i),
                send_sem=sends.at[lane, i],
                recv_sem=recvs.at[owner, i],
                device_id={"dp": to},
            )

        def landed(owner, i):
            move(0, owner, i, mine).wait_recv()

        def spread_line(i):
            move(1, mine, i, right, own(i)).start()
            move(2, mine, i, left, own(i)).start()

        def spread_face(i):
            move(0, mine, i, facing, own(i)).start()

        def pass_on(i):
            turn = 2 * lax.rem(i, 2) - 1
            landed(peer(turn), i)
            move(3, peer(turn), i, peer(-turn)).start()

        def relay(i):
            landed(facing, i)
            move(4, facing, i, right).start()
            move(5, facing, i, left).start()

        def cross(i):
            turn = 2 * lax.rem(i, 2) - 1

            @pl.when(crosses(i))
            def _():
                landed(far, i)
                move(6, far, i, facing).start()

            @pl.when(jnp.logical_not(crosses(i)))
            def _():
                landed(peer(turn, True), i)
                move(6, peer(turn, True), i, peer(-turn)).start()

        def finish(i):
            turn = 2 * lax.rem(i, 2) - 1
            landed(peer(-turn), i)
            landed(peer(-turn, True), i)
            landed(peer(2, True), i)

            @pl.when(crosses(i))
            def _():
                landed(peer(turn, True), i)

            @pl.when(jnp.logical_not(crosses(i)))
            def _():
                landed(far, i)

        def sent(i):
            for lane in range(7):
                move(lane, mine, i, mine).wait_send()

        return spread_line, spread_face, pass_on, relay, cross, finish, sent

    def each(count, *steps, first=0):
        for step in steps:

            def one(i, carry, step=step):
                step(i)
                return carry

            lax.fori_loop(first, first + count, one, 0)

    def weight_place(owner, i):
        return weight.at[pl.ds(pl.multiple_of(owner * shard + i * piece, 16), piece)]

    weight_spread = spread_over(
        weight_place,
        lambda i: shard_ref.at[pl.ds(pl.multiple_of(i * piece, 16), piece)],
        weight_send,
        weight_recv,
        lambda i: i >= 0,
    )

    def grad_place(owner, i):
        pair = pl.ds(2 * lax.rem(i, pairs), 2)
        half = pl.ds(pl.multiple_of((i // pairs) * (width // 2), 128), width // 2)
        return gathered.at[owner, pair, :, half]

    (
        grad_line,
        grad_face,
        grad_pass,
        grad_relay,
        grad_cross,
        grad_finish,
        grad_sent,
    ) = spread_over(
        grad_place,
        lambda i: grad_place(mine, i),
        grad_send,
        grad_recv,
        lambda i: (me < 2) | (lax.rem(i // 2, 2) == 0),
    )

    def ahead(i):
        return pltpu.make_async_remote_copy(
            src_ref=outputs.at[i],
            dst_ref=arrived.at[i],
            send_sem=ahead_send.at[i],
            recv_sem=ahead_recv.at[i],
            device_id={"section": after},
        )

    def ahead_part(i, k):
        part = pl.ds(k * PART, PART)
        return pltpu.make_async_remote_copy(
            src_ref=outputs.at[i, :, part],
            dst_ref=arrived.at[i, :, part],
            send_sem=part_send.at[0, i, k],
            recv_sem=part_recv.at[0, i, k],
            device_id={"section": after},
        )

    def back(i):
        return pltpu.make_async_remote_copy(
            src_ref=grads_out.at[i],
            dst_ref=grads_in.at[i],
            send_sem=back_send.at[i],
            recv_sem=back_recv.at[i],
            device_id={"section": before},
        )

    def back_part(i, k):
        part = pl.ds(k * PART, PART)
        return pltpu.make_async_remote_copy(
            src_ref=grads_out.at[i, :, part],
            dst_ref=grads_in.at[i, :, part],
            send_sem=part_send.at[1, i, k],
            recv_sem=part_recv.at[1, i, k],
            device_id={"section": before},
        )

    def shadow(i):
        return pltpu.make_async_remote_copy(
            src_ref=outputs.at[i],
            dst_ref=shadow_ref.at[i],
            send_sem=shadow_send.at[i],
            recv_sem=shadow_recv.at[i],
            device_id={"section": before},
        )

    def window(owner):
        start = (owner // 2) * (2 * shard) + lax.rem(owner, 2) * (2 * shard - WINDOW)
        return normed_all.at[:, :, pl.ds(pl.multiple_of(start, 128), WINDOW)]

    def unit(step):
        to = lax.rem(mine + step, replicas)
        return pltpu.make_async_remote_copy(
            src_ref=window(to),
            dst_ref=units.at[mine],
            send_sem=unit_send.at[step],
            recv_sem=unit_recv.at[step],
            device_id={"dp": to},
        )

    def columns(k):
        return pl.ds(pl.multiple_of(k * CHUNK, CHUNK), CHUNK)

    def fresh_move(k):
        return pltpu.make_async_remote_copy(
            src_ref=fresh.at[:, columns(k)],
            dst_ref=shadow_weight_ref.at[:, columns(k)],
            send_sem=fresh_send.at[k],
            recv_sem=fresh_recv.at[k],
            device_id={"section": before},
        )

    def flip(k):
        row, column = columns(k // blocks), columns(lax.rem(k, blocks))
        flipped[column, row] = weight[row, column].T

    each(PIECES, *weight_spread)
    loads[0].wait()
    loads[1].start()
    loads[2].start()

    @pl.when(me == 0)
    def _():
        arrived[...] = inputs_ref[...]

    @pl.when(me == sections - 1)
    def _():
        grads_in[...] = cotangent_ref[...]

    @pl.when(me >= sections // 2)
    def _():
        each(blocks * blocks, flip)

    def keep(i, at, v, t):
        part = pl.ds(at, PART)
        pre_acts[i, :, part] = v
        slope = 0.5 * (1.0 + t) + 0.5 * v * (1.0 - t * t) * tanh_coef * (
            1.0 + 3.0 * cubic_coef * v * v
        )
        slopes[i, :, part] = branch_scale * slope

    def finish_output(i, at, v):
        part = pl.ds(at, PART)
        t = jnp.tanh(tanh_coef * (v + cubic_coef * v * v * v))
        out = arrived[i, :, part].astype(jnp.float32) + branch_scale * (0.5 * v * (1.0 + t))
        outputs[i, :, part] = out.astype(jnp.bfloat16)
        return t

    def rms_scale(squares):
        return lax.rsqrt(squares * (1.0 / width) + norm_eps)

    def forward_spread(i):
        ahead(i).wait_recv()
        current = arrived[i].astype(jnp.float32)
        scale = rms_scale(jnp.sum(current * current, axis=-1, keepdims=True))
        raw = arrived[i]

        def product(at):
            return jnp.dot(raw, weight[:, pl.ds(at, PART)], preferred_element_type=jnp.float32)

        following = product(0)
        for at in range(0, width, PART):
            v = following * scale
            if at + PART < width:
                following = product(at + PART)
            t = finish_output(i, at, v)

            @pl.when(me < sections - 1)
            def _():
                ahead_part(i, at // PART).start()

            keep(i, at, v, t)
        scales[i] = jnp.broadcast_to(scale, (rows, 128))
        normed_all[i] = (current * scale).astype(jnp.bfloat16)
        shadow(i).start()

    def forward_collect(i):
        squares = jnp.zeros((rows, 1), jnp.float32)
        for at in range(0, width, PART):
            part = pl.ds(at, PART)

            @pl.when(me > 0)
            def _():
                ahead_part(i, at // PART).wait_recv()

            raw = arrived[i, :, part]
            current = raw.astype(jnp.float32)
            squares += jnp.sum(current * current, axis=-1, keepdims=True)
            product = jnp.dot(raw, weight[part, :], preferred_element_type=jnp.float32)
            if at == 0:
                sums[...] = product
            else:
                sums[...] += product
        scale = rms_scale(squares)
        values = []
        for at in range(0, width, PART):
            v = sums[:, pl.ds(at, PART)] * scale
            values.append((at, v, finish_output(i, at, v)))
        ahead(i).start()
        shadow(i).start()
        for at, v, t in values:
            keep(i, at, v, t)
        scales[i] = jnp.broadcast_to(scale, (rows, 128))
        normed_all[i] = (arrived[i].astype(jnp.float32) * scale).astype(jnp.bfloat16)

    odd = lax.rem(me, 2)

    @pl.when(odd == 1)
    def _():
        each(micro, forward_spread)

    @pl.when(odd == 0)
    def _():
        each(micro, forward_collect)

    def send_units():
        for step in range(1, replicas):
            unit(step).start()
        units[mine] = window(mine)[...]

    def flip_units():
        for step in range(1, replicas):
            unit(step).wait_recv()

        def one(k):
            block = units[k].reshape(tokens, WINDOW)
            units_flipped[:, pl.ds(pl.multiple_of(k * tokens, tokens), tokens)] = block.T

        each(replicas, one)

    @pl.when(me < sections // 2)
    def _():
        each(blocks * blocks, flip)
        send_units()
        flip_units()

    def finish_grad(i, at, g, scale, pull):
        part = pl.ds(at, PART)
        a = arrived[i, :, part].astype(jnp.float32)
        total = grads_in[i, :, part].astype(jnp.float32) + scale * g - pull * a
        grads_out[i, :, part] = total.astype(jnp.bfloat16)

    def push_grads(i):
        @pl.when(lax.rem(i, 2) == 1)
        def _():
            for half in range(2):
                grad_line(half * pairs + i // 2)

                @pl.when(me < 2)
                def _(half=half):
                    grad_face(half * pairs + i // 2)

    def backward_spread(i):
        back(i).wait_recv()
        grad_pre = (grads_in[i].astype(jnp.float32) * slopes[i]).astype(jnp.bfloat16)
        gathered[mine, i] = grad_pre

        @pl.when(me > 0)
        def _():
            overlap = jnp.sum(
                grad_pre.astype(jnp.float32) * pre_acts[i], axis=-1, keepdims=True
            ) * (1.0 / width)
            scale = scales[i][:, :1]
            pull = scale * scale * overlap

            def product(at):
                return jnp.dot(
                    grad_pre, flipped[:, pl.ds(at, PART)], preferred_element_type=jnp.float32
                )

            following = product(0)
            for at in range(0, width, PART):
                g = following
                if at + PART < width:
                    following = product(at + PART)
                finish_grad(i, at, g, scale, pull)
                back_part(i, at // PART).start()
        push_grads(i)

    def backward_collect(i):
        overlap = jnp.zeros((rows, 1), jnp.float32)
        for at in range(0, width, PART):
            part = pl.ds(at, PART)

            @pl.when(me < sections - 1)
            def _():
                back_part(i, at // PART).wait_recv()

            grad_pre = (grads_in[i, :, part].astype(jnp.float32) * slopes[i, :, part]).astype(
                jnp.bfloat16
            )
            gathered[mine, i, :, part] = grad_pre
            overlap += jnp.sum(
                grad_pre.astype(jnp.float32) * pre_acts[i, :, part], axis=-1, keepdims=True
            )
            product = jnp.dot(grad_pre, flipped[part, :], preferred_element_type=jnp.float32)
            if at == 0:
                sums[...] = product
            else:
                sums[...] += product
        scale = scales[i][:, :1]
        pull = scale * scale * overlap * (1.0 / width)
        for at in range(0, width, PART):
            finish_grad(i, at, sums[:, pl.ds(at, PART)], scale, pull)
        back(i).start()
        push_grads(i)

    @pl.when(odd == 0)
    def _():
        each(micro, backward_spread)

    @pl.when(odd == 1)
    def _():
        each(micro, backward_collect)

    @pl.when((me > 0) & (me < sections - APART))
    def _():
        pl.semaphore_signal(passed, inc=1, device_id={"section": later})

    @pl.when(me > APART)
    def _():
        pl.semaphore_wait(passed, 1)

    @pl.when(me >= 2)
    def _():
        each(micro, grad_face)

    each(micro, grad_pass, grad_relay, grad_cross)

    @pl.when(me >= sections // 2)
    def _():
        send_units()
        flip_units()

    loads[1].wait()
    loads[2].wait()
    skip = lax.rem(mine, 2) * (WINDOW - shard)
    own_rows = mine * shard
    strip = shard // 5

    def step_weights(k):
        part = columns(k)
        grads = gathered[:, :, :, part].reshape(replicas * tokens, CHUNK)
        stage[...] = jnp.dot(units_flipped[...], grads, preferred_element_type=jnp.float32) * (
            1.0 / (replicas * tokens)
        )

        def adam(j):
            here = pl.ds(pl.multiple_of(j * strip, strip), strip)
            gradient = stage[pl.ds(pl.multiple_of(skip + j * strip, 16), strip), :]
            one = beta_one * moment_one[here, part] + (1.0 - beta_one) * gradient
            two = beta_two * moment_two[here, part] + (1.0 - beta_two) * gradient * gradient
            corrected_one = one * (1.0 / (1.0 - beta_one**step_count))
            corrected_two = two * (1.0 / (1.0 - beta_two**step_count))
            direction = corrected_one / (jnp.sqrt(corrected_two) + adam_eps)
            old = weight[pl.ds(pl.multiple_of(own_rows + j * strip, 16), strip), part]
            update_ref[here, part] = direction.astype(jnp.bfloat16)
            fresh[here, part] = (old.astype(jnp.float32) - learn_rate * direction).astype(
                jnp.bfloat16
            )

        each(5, adam)
        fresh_move(k).start()

    for half in range(2):
        each(pairs, grad_finish, first=half * pairs)
        each(blocks // 2, step_weights, first=half * (blocks // 2))

    def settle(i):
        @pl.when(odd == 0)
        def _():
            ahead(i).wait_send()

        @pl.when(odd == 1)
        def _():
            back(i).wait_send()

        for k in range(width // PART):

            @pl.when((odd == 1) & (me < sections - 1))
            def _(k=k):
                ahead_part(i, k).wait_send()

            @pl.when((odd == 0) & (me > 0))
            def _(k=k):
                back_part(i, k).wait_send()

        shadow(i).wait_send()
        shadow(i).wait_recv()

    def settle_fresh(k):
        fresh_move(k).wait_send()
        fresh_move(k).wait_recv()

    each(micro, settle, grad_sent)
    for step in range(1, replicas):
        unit(step).wait_send()
    each(blocks, settle_fresh)


def on_device(inputs, cotangent, weights, adam_m, adam_v):
    sections = lax.axis_size("section")
    replicas = lax.axis_size("dp")
    tokens, width = inputs.shape
    shard = width // replicas
    rows = tokens // MICRO
    block = (MICRO, rows, width)
    low = jnp.bfloat16
    wide = jnp.float32
    in_vmem = pl.BlockSpec(memory_space=pltpu.VMEM)
    anywhere = pl.BlockSpec(memory_space=pl.ANY)
    dma = pltpu.SemaphoreType.DMA
    update, shadow_weight, shadow_output = pl.pallas_call(
        functools.partial(chain_kernel, sections, replicas),
        out_shape=(
            jax.ShapeDtypeStruct((shard, width), low),
            jax.ShapeDtypeStruct((shard, width), low),
            jax.ShapeDtypeStruct(block, low),
        ),
        in_specs=[in_vmem, in_vmem, anywhere, anywhere, anywhere],
        out_specs=(in_vmem, anywhere, anywhere),
        scratch_shapes=[
            pltpu.VMEM((width, width), low),
            pltpu.VMEM((width, width), low),
            pltpu.VMEM(block, low),
            pltpu.VMEM(block, low),
            pltpu.VMEM(block, low),
            pltpu.VMEM(block, low),
            pltpu.VMEM(block, wide),
            pltpu.VMEM(block, wide),
            pltpu.VMEM((MICRO, rows, 128), wide),
            pltpu.VMEM(block, low),
            pltpu.VMEM((replicas, MICRO, rows, WINDOW), low),
            pltpu.VMEM((WINDOW, replicas * tokens), low),
            pltpu.VMEM((replicas,) + block, low),
            pltpu.VMEM((shard, width), wide),
            pltpu.VMEM((shard, width), wide),
            pltpu.VMEM((shard, width), low),
            pltpu.VMEM((WINDOW, CHUNK), wide),
            pltpu.VMEM((rows, width), wide),
            dma((3,)),
        ]
        + [dma((MICRO,))] * 6
        + [
            dma((7, PIECES)),
            dma((replicas, PIECES)),
            dma((7, MICRO)),
            dma((replicas, MICRO)),
            dma((replicas,)),
            dma((replicas,)),
            dma((width // CHUNK,)),
            dma((width // CHUNK,)),
            dma((2, MICRO, width // PART)),
            dma((2, MICRO, width // PART)),
            pltpu.SemaphoreType.REGULAR,
        ],
        compiler_params=pltpu.CompilerParams(
            collective_id=0, has_side_effects=True, vmem_limit_bytes=60 * 2**20
        ),
        cost_estimate=pl.CostEstimate(
            flops=6 * tokens * width * width,
            bytes_accessed=16 * shard * width,
            transcendentals=tokens * width,
        ),
    )(
        inputs.reshape(block),
        cotangent.reshape(block),
        weights[0],
        adam_m[0],
        adam_v[0],
    )
    return (update[None], shadow_weight[None], shadow_output.reshape(1, tokens, width))


def solution(mesh):
    in_specs = (
        P("dp", None),
        P("dp", None),
        P("section", "dp", None),
        P("section", "dp", None),
        P("section", "dp", None),
    )
    out_specs = (P("section", "dp", None), P("section", "dp", None), P("section", "dp", None))
    return jax.shard_map(
        on_device, mesh=mesh, in_specs=in_specs, out_specs=out_specs, check_vma=False
    )
```

```python
import functools
import jax
import jax.numpy as jnp
from jax import lax
from jax.experimental import pallas as pl
from jax.experimental.pallas import tpu as pltpu
from jax.sharding import PartitionSpec as P

MICRO = 8
CHUNK = 256
PART = 512
APART = 2
PIECES = 4
WINDOW = 384

branch_scale = 0.5
norm_eps = 1e-05
beta_one = 0.9
beta_two = 0.95
adam_eps = 1e-08
learn_rate = 0.01
step_count = 4.0
tanh_coef = 0.7978845608028654
cubic_coef = 0.044715


def chain_kernel(
    sections,
    replicas,
    inputs_ref,
    cotangent_ref,
    shard_ref,
    moment_one_ref,
    moment_two_ref,
    update_ref,
    shadow_weight_ref,
    shadow_ref,
    weight,
    flipped,
    arrived,
    outputs,
    grads_in,
    grads_out,
    pre_acts,
    slopes,
    scales,
    normed_all,
    units,
    units_flipped,
    gathered,
    moment_one,
    moment_two,
    fresh,
    stage,
    sums,
    load_sem,
    ahead_send,
    ahead_recv,
    back_send,
    back_recv,
    shadow_send,
    shadow_recv,
    weight_send,
    weight_recv,
    grad_send,
    grad_recv,
    unit_send,
    unit_recv,
    fresh_send,
    fresh_recv,
    part_send,
    part_recv,
    passed,
):
    micro, rows, width = arrived.shape
    shard = width // replicas
    piece = shard // PIECES
    ring = replicas // 2
    tokens = micro * rows
    blocks = width // CHUNK
    pairs = micro // 2
    me = lax.axis_index("section")
    mine = lax.axis_index("dp")
    after = lax.rem(me + 1, sections)
    before = lax.rem(me + sections - 1, sections)
    line, side = mine // 2, lax.rem(mine, 2)

    def peer(step, across=False):
        return lax.rem(line + step + ring, ring) * 2 + (1 - side if across else side)

    right, left, facing, far = peer(1), peer(-1), peer(0, True), peer(2)

    loads = [
        pltpu.make_async_copy(
            shard_ref,
            weight.at[pl.ds(pl.multiple_of(mine * shard, 16), shard)],
            load_sem.at[0],
        ),
        pltpu.make_async_copy(moment_one_ref, moment_one, load_sem.at[1]),
        pltpu.make_async_copy(moment_two_ref, moment_two, load_sem.at[2]),
    ]
    loads[0].start()
    barrier = pltpu.get_barrier_semaphore()
    later = lax.rem(me + APART, sections)
    earlier = lax.rem(me + sections - APART, sections)
    for other in (before, after, earlier, later):
        pl.semaphore_signal(barrier, inc=1, device_id={"section": other})
    for step in range(1, replicas):
        pl.semaphore_signal(barrier, inc=1, device_id={"dp": lax.rem(mine + step, replicas)})
    pl.semaphore_wait(barrier, replicas + 3)

    def spread_over(place, own, sends, recvs, crosses):
        def move(lane, owner, i, to, source=None):
            return pltpu.make_async_remote_copy(
                src_ref=place(owner, i) if source is None else source,
                dst_ref=place(owner, i),
                send_sem=sends.at[lane, i],
                recv_sem=recvs.at[owner, i],
                device_id={"dp": to},
            )

        def landed(owner, i):
            move(0, owner, i, mine).wait_recv()

        def spread_line(i):
            move(1, mine, i, right, own(i)).start()
            move(2, mine, i, left, own(i)).start()

        def spread_face(i):
            move(0, mine, i, facing, own(i)).start()

        def pass_on(i):
            turn = 2 * lax.rem(i, 2) - 1
            landed(peer(turn), i)
            move(3, peer(turn), i, peer(-turn)).start()

        def relay(i):
            landed(facing, i)
            move(4, facing, i, right).start()
            move(5, facing, i, left).start()

        def cross(i):
            turn = 2 * lax.rem(i, 2) - 1

            @pl.when(crosses(i))
            def _():
                landed(far, i)
                move(6, far, i, facing).start()

            @pl.when(jnp.logical_not(crosses(i)))
            def _():
                landed(peer(turn, True), i)
                move(6, peer(turn, True), i, peer(-turn)).start()

        def finish(i):
            turn = 2 * lax.rem(i, 2) - 1
            landed(peer(-turn), i)
            landed(peer(-turn, True), i)
            landed(peer(2, True), i)

            @pl.when(crosses(i))
            def _():
                landed(peer(turn, True), i)

            @pl.when(jnp.logical_not(crosses(i)))
            def _():
                landed(far, i)

        def sent(i):
            for lane in range(7):
                move(lane, mine, i, mine).wait_send()

        return spread_line, spread_face, pass_on, relay, cross, finish, sent

    def each(count, *steps, first=0):
        for step in steps:

            def one(i, carry, step=step):
                step(i)
                return carry

            lax.fori_loop(first, first + count, one, 0)

    def weight_place(owner, i):
        return weight.at[pl.ds(pl.multiple_of(owner * shard + i * piece, 16), piece)]

    weight_spread = spread_over(
        weight_place,
        lambda i: shard_ref.at[pl.ds(pl.multiple_of(i * piece, 16), piece)],
        weight_send,
        weight_recv,
        lambda i: i >= 0,
    )

    def grad_place(owner, i):
        pair = pl.ds(2 * lax.rem(i, pairs), 2)
        half = pl.ds(pl.multiple_of((i // pairs) * (width // 2), 128), width // 2)
        return gathered.at[owner, pair, :, half]

    (
        grad_line,
        grad_face,
        grad_pass,
        grad_relay,
        grad_cross,
        grad_finish,
        grad_sent,
    ) = spread_over(
        grad_place,
        lambda i: grad_place(mine, i),
        grad_send,
        grad_recv,
        lambda i: (me < 2) | (lax.rem(i // 2, 2) == 0),
    )

    def ahead(i):
        return pltpu.make_async_remote_copy(
            src_ref=outputs.at[i],
            dst_ref=arrived.at[i],
            send_sem=ahead_send.at[i],
            recv_sem=ahead_recv.at[i],
            device_id={"section": after},
        )

    def ahead_part(i, k):
        part = pl.ds(k * PART, PART)
        return pltpu.make_async_remote_copy(
            src_ref=outputs.at[i, :, part],
            dst_ref=arrived.at[i, :, part],
            send_sem=part_send.at[0, i, k],
            recv_sem=part_recv.at[0, i, k],
            device_id={"section": after},
        )

    def back(i):
        return pltpu.make_async_remote_copy(
            src_ref=grads_out.at[i],
            dst_ref=grads_in.at[i],
            send_sem=back_send.at[i],
            recv_sem=back_recv.at[i],
            device_id={"section": before},
        )

    def back_part(i, k):
        part = pl.ds(k * PART, PART)
        return pltpu.make_async_remote_copy(
            src_ref=grads_out.at[i, :, part],
            dst_ref=grads_in.at[i, :, part],
            send_sem=part_send.at[1, i, k],
            recv_sem=part_recv.at[1, i, k],
            device_id={"section": before},
        )

    def shadow(i):
        return pltpu.make_async_remote_copy(
            src_ref=outputs.at[i],
            dst_ref=shadow_ref.at[i],
            send_sem=shadow_send.at[i],
            recv_sem=shadow_recv.at[i],
            device_id={"section": before},
        )

    def window(owner):
        start = (owner // 2) * (2 * shard) + lax.rem(owner, 2) * (2 * shard - WINDOW)
        return normed_all.at[:, :, pl.ds(pl.multiple_of(start, 128), WINDOW)]

    def unit(step):
        to = lax.rem(mine + step, replicas)
        return pltpu.make_async_remote_copy(
            src_ref=window(to),
            dst_ref=units.at[mine],
            send_sem=unit_send.at[step],
            recv_sem=unit_recv.at[step],
            device_id={"dp": to},
        )

    def columns(k):
        return pl.ds(pl.multiple_of(k * CHUNK, CHUNK), CHUNK)

    def fresh_move(k):
        return pltpu.make_async_remote_copy(
            src_ref=fresh.at[:, columns(k)],
            dst_ref=shadow_weight_ref.at[:, columns(k)],
            send_sem=fresh_send.at[k],
            recv_sem=fresh_recv.at[k],
            device_id={"section": before},
        )

    def flip(k):
        row, column = columns(k // blocks), columns(lax.rem(k, blocks))
        flipped[column, row] = weight[row, column].T

    each(PIECES, *weight_spread)
    loads[0].wait()
    loads[1].start()
    loads[2].start()

    @pl.when(me == 0)
    def _():
        arrived[...] = inputs_ref[...]

    @pl.when(me == sections - 1)
    def _():
        grads_in[...] = cotangent_ref[...]

    @pl.when(me >= sections // 2)
    def _():
        each(blocks * blocks, flip)

    def keep(i, at, v, t):
        part = pl.ds(at, PART)
        pre_acts[i, :, part] = v
        slope = 0.5 * (1.0 + t) + 0.5 * v * (1.0 - t * t) * tanh_coef * (
            1.0 + 3.0 * cubic_coef * v * v
        )
        slopes[i, :, part] = branch_scale * slope

    def finish_output(i, at, v):
        part = pl.ds(at, PART)
        t = jnp.tanh(tanh_coef * (v + cubic_coef * v * v * v))
        out = arrived[i, :, part].astype(jnp.float32) + branch_scale * (0.5 * v * (1.0 + t))
        outputs[i, :, part] = out.astype(jnp.bfloat16)
        return t

    def rms_scale(squares):
        return lax.rsqrt(squares * (1.0 / width) + norm_eps)

    def lanes(values):
        total = values[:, :128]
        for at in range(128, values.shape[1], 128):
            total += values[:, at : at + 128]
        return total

    def row_total(partial):
        return jnp.sum(partial, axis=-1, keepdims=True)

    def forward_spread(last, i):
        ahead(i).wait_recv()
        raw = arrived[i]

        def product(at):
            return jnp.dot(raw, weight[:, pl.ds(at, PART)], preferred_element_type=jnp.float32)

        following = product(0)
        current = raw.astype(jnp.float32)
        scale = rms_scale(row_total(lanes(current * current)))
        scales[i] = jnp.broadcast_to(scale, (rows, 128))
        for at in range(0, width, PART):
            v = following * scale
            if at + PART < width:
                following = product(at + PART)
            t = finish_output(i, at, v)
            if at + PART < width:
                keep(i, at, v, t)
            if not last:
                ahead_part(i, at // PART).start()
        keep(i, at, v, t)
        normed_all[i] = (arrived[i].astype(jnp.float32) * scale).astype(jnp.bfloat16)

    def forward_collect(first, i):
        squares = jnp.zeros((rows, 128), jnp.float32)
        for at in range(0, width - PART, PART):
            part = pl.ds(at, PART)
            if not first:
                ahead_part(i, at // PART).wait_recv()
            raw = arrived[i, :, part]
            current = raw.astype(jnp.float32)
            squares += lanes(current * current)
            product = jnp.dot(raw, weight[part, :], preferred_element_type=jnp.float32)
            if at == 0:
                sums[...] = product
            else:
                sums[...] += product
        end = pl.ds(width - PART, PART)
        if not first:
            ahead_part(i, width // PART - 1).wait_recv()
        raw = arrived[i, :, end]

        def product(at):
            part = pl.ds(at, PART)
            return sums[:, part] + jnp.dot(
                raw, weight[end, part], preferred_element_type=jnp.float32
            )

        current = raw.astype(jnp.float32)
        scale = rms_scale(row_total(squares + lanes(current * current)))
        values = []
        following = product(0)
        for at in range(0, width, PART):
            v = following * scale
            if at + PART < width:
                following = product(at + PART)
            values.append((at, v, finish_output(i, at, v)))
        ahead(i).start()
        for at, v, t in values:
            keep(i, at, v, t)
        scales[i] = jnp.broadcast_to(scale, (rows, 128))
        normed_all[i] = (arrived[i].astype(jnp.float32) * scale).astype(jnp.bfloat16)

    odd = lax.rem(me, 2)

    @pl.when((odd == 1) & (me < sections - 1))
    def _():
        each(micro, functools.partial(forward_spread, False))

    @pl.when(me == sections - 1)
    def _():
        each(micro, functools.partial(forward_spread, True))

    @pl.when((odd == 0) & (me > 0))
    def _():
        each(micro, functools.partial(forward_collect, False))

    @pl.when(me == 0)
    def _():
        each(micro, functools.partial(forward_collect, True))

    def send_units():
        for step in range(1, replicas):
            unit(step).start()
        units[mine] = window(mine)[...]

    def flip_units():
        for step in range(1, replicas):
            unit(step).wait_recv()

        def one(k):
            block = units[k].reshape(tokens, WINDOW)
            units_flipped[:, pl.ds(pl.multiple_of(k * tokens, tokens), tokens)] = block.T

        each(replicas, one)

    @pl.when(me < sections // 2)
    def _():
        each(micro, lambda i: shadow(i).start())
        each(blocks * blocks, flip)
        send_units()
        flip_units()

    def finish_grad(i, at, g, scale, pull):
        part = pl.ds(at, PART)
        a = arrived[i, :, part].astype(jnp.float32)
        total = grads_in[i, :, part].astype(jnp.float32) + scale * g - pull * a
        grads_out[i, :, part] = total.astype(jnp.bfloat16)

    def push_grads(i):
        @pl.when(lax.rem(i, 2) == 1)
        def _():
            for half in range(2):
                grad_line(half * pairs + i // 2)

                @pl.when(me < 2)
                def _(half=half):
                    grad_face(half * pairs + i // 2)

    def backward_spread(i):
        back(i).wait_recv()
        grad_pre = (grads_in[i].astype(jnp.float32) * slopes[i]).astype(jnp.bfloat16)
        gathered[mine, i] = grad_pre

        @pl.when(me > 0)
        def _():
            overlap = jnp.sum(
                grad_pre.astype(jnp.float32) * pre_acts[i], axis=-1, keepdims=True
            ) * (1.0 / width)
            scale = scales[i][:, :1]
            pull = scale * scale * overlap

            def product(at):
                return jnp.dot(
                    grad_pre, flipped[:, pl.ds(at, PART)], preferred_element_type=jnp.float32
                )

            following = product(0)
            for at in range(0, width, PART):
                g = following
                if at + PART < width:
                    following = product(at + PART)
                finish_grad(i, at, g, scale, pull)
                back_part(i, at // PART).start()
        push_grads(i)

    def backward_collect(first, i):
        overlap = jnp.zeros((rows, 128), jnp.float32)

        def grad_part(at):
            part = pl.ds(at, PART)
            if not first:
                back_part(i, at // PART).wait_recv()
            grad_pre = (grads_in[i, :, part].astype(jnp.float32) * slopes[i, :, part]).astype(
                jnp.bfloat16
            )
            gathered[mine, i, :, part] = grad_pre
            return grad_pre, lanes(grad_pre.astype(jnp.float32) * pre_acts[i, :, part])

        for at in range(0, width - PART, PART):
            grad_pre, extra = grad_part(at)
            overlap += extra
            product = jnp.dot(
                grad_pre, flipped[pl.ds(at, PART), :], preferred_element_type=jnp.float32
            )
            if at == 0:
                sums[...] = product
            else:
                sums[...] += product
        grad_pre, extra = grad_part(width - PART)
        end = pl.ds(width - PART, PART)

        def finish_product(at):
            part = pl.ds(at, PART)
            return sums[:, part] + jnp.dot(
                grad_pre, flipped[end, part], preferred_element_type=jnp.float32
            )

        following = finish_product(0)
        scale = scales[i][:, :1]
        pull = scale * scale * row_total(overlap + extra) * (1.0 / width)
        for at in range(0, width, PART):
            g = following
            if at + PART < width:
                following = finish_product(at + PART)
            finish_grad(i, at, g, scale, pull)
        back(i).start()
        push_grads(i)

    @pl.when(odd == 0)
    def _():
        each(micro, backward_spread)

    @pl.when((odd == 1) & (me < sections - 1))
    def _():
        each(micro, functools.partial(backward_collect, False))

    @pl.when(me == sections - 1)
    def _():
        each(micro, functools.partial(backward_collect, True))

    @pl.when((me > 0) & (me < sections - APART))
    def _():
        pl.semaphore_signal(passed, inc=1, device_id={"section": later})

    @pl.when(me > APART)
    def _():
        pl.semaphore_wait(passed, 1)

    @pl.when(me >= 2)
    def _():
        each(micro, grad_face)

    each(micro, grad_pass, grad_relay, grad_cross)

    @pl.when(me >= sections // 2)
    def _():
        each(micro, lambda i: shadow(i).start())
        send_units()
        flip_units()

    loads[1].wait()
    loads[2].wait()
    skip = lax.rem(mine, 2) * (WINDOW - shard)
    own_rows = mine * shard
    strip = shard // 5

    def step_weights(k):
        part = columns(k)
        grads = gathered[:, :, :, part].reshape(replicas * tokens, CHUNK)
        stage[...] = jnp.dot(units_flipped[...], grads, preferred_element_type=jnp.float32) * (
            1.0 / (replicas * tokens)
        )

        def adam(j):
            here = pl.ds(pl.multiple_of(j * strip, strip), strip)
            gradient = stage[pl.ds(pl.multiple_of(skip + j * strip, 16), strip), :]
            one = beta_one * moment_one[here, part] + (1.0 - beta_one) * gradient
            two = beta_two * moment_two[here, part] + (1.0 - beta_two) * gradient * gradient
            corrected_one = one * (1.0 / (1.0 - beta_one**step_count))
            corrected_two = two * (1.0 / (1.0 - beta_two**step_count))
            direction = corrected_one / (jnp.sqrt(corrected_two) + adam_eps)
            old = weight[pl.ds(pl.multiple_of(own_rows + j * strip, 16), strip), part]
            update_ref[here, part] = direction.astype(jnp.bfloat16)
            fresh[here, part] = (old.astype(jnp.float32) - learn_rate * direction).astype(
                jnp.bfloat16
            )

        each(5, adam)
        fresh_move(k).start()

    for half in range(2):
        each(pairs, grad_finish, first=half * pairs)
        each(blocks // 2, step_weights, first=half * (blocks // 2))

    def settle(i):
        @pl.when(odd == 0)
        def _():
            ahead(i).wait_send()

        @pl.when(odd == 1)
        def _():
            back(i).wait_send()

        for k in range(width // PART):

            @pl.when((odd == 1) & (me < sections - 1))
            def _(k=k):
                ahead_part(i, k).wait_send()

            @pl.when((odd == 0) & (me > 0))
            def _(k=k):
                back_part(i, k).wait_send()

        shadow(i).wait_send()
        shadow(i).wait_recv()

    def settle_fresh(k):
        fresh_move(k).wait_send()
        fresh_move(k).wait_recv()

    each(micro, settle, grad_sent)
    for step in range(1, replicas):
        unit(step).wait_send()
    each(blocks, settle_fresh)


def on_device(inputs, cotangent, weights, adam_m, adam_v):
    sections = lax.axis_size("section")
    replicas = lax.axis_size("dp")
    tokens, width = inputs.shape
    shard = width // replicas
    rows = tokens // MICRO
    block = (MICRO, rows, width)
    low = jnp.bfloat16
    wide = jnp.float32
    in_vmem = pl.BlockSpec(memory_space=pltpu.VMEM)
    anywhere = pl.BlockSpec(memory_space=pl.ANY)
    dma = pltpu.SemaphoreType.DMA
    update, shadow_weight, shadow_output = pl.pallas_call(
        functools.partial(chain_kernel, sections, replicas),
        out_shape=(
            jax.ShapeDtypeStruct((shard, width), low),
            jax.ShapeDtypeStruct((shard, width), low),
            jax.ShapeDtypeStruct(block, low),
        ),
        in_specs=[in_vmem, in_vmem, anywhere, anywhere, anywhere],
        out_specs=(in_vmem, anywhere, anywhere),
        scratch_shapes=[
            pltpu.VMEM((width, width), low),
            pltpu.VMEM((width, width), low),
            pltpu.VMEM(block, low),
            pltpu.VMEM(block, low),
            pltpu.VMEM(block, low),
            pltpu.VMEM(block, low),
            pltpu.VMEM(block, wide),
            pltpu.VMEM(block, wide),
            pltpu.VMEM((MICRO, rows, 128), wide),
            pltpu.VMEM(block, low),
            pltpu.VMEM((replicas, MICRO, rows, WINDOW), low),
            pltpu.VMEM((WINDOW, replicas * tokens), low),
            pltpu.VMEM((replicas,) + block, low),
            pltpu.VMEM((shard, width), wide),
            pltpu.VMEM((shard, width), wide),
            pltpu.VMEM((shard, width), low),
            pltpu.VMEM((WINDOW, CHUNK), wide),
            pltpu.VMEM((rows, width), wide),
            dma((3,)),
        ]
        + [dma((MICRO,))] * 6
        + [
            dma((7, PIECES)),
            dma((replicas, PIECES)),
            dma((7, MICRO)),
            dma((replicas, MICRO)),
            dma((replicas,)),
            dma((replicas,)),
            dma((width // CHUNK,)),
            dma((width // CHUNK,)),
            dma((2, MICRO, width // PART)),
            dma((2, MICRO, width // PART)),
            pltpu.SemaphoreType.REGULAR,
        ],
        compiler_params=pltpu.CompilerParams(
            collective_id=0, has_side_effects=True, vmem_limit_bytes=60 * 2**20
        ),
        cost_estimate=pl.CostEstimate(
            flops=6 * tokens * width * width,
            bytes_accessed=16 * shard * width,
            transcendentals=tokens * width,
        ),
    )(
        inputs.reshape(block),
        cotangent.reshape(block),
        weights[0],
        adam_m[0],
        adam_v[0],
    )
    return (update[None], shadow_weight[None], shadow_output.reshape(1, tokens, width))


def solution(mesh):
    in_specs = (
        P("dp", None),
        P("dp", None),
        P("section", "dp", None),
        P("section", "dp", None),
        P("section", "dp", None),
    )
    out_specs = (P("section", "dp", None), P("section", "dp", None), P("section", "dp", None))
    return jax.shard_map(
        on_device, mesh=mesh, in_specs=in_specs, out_specs=out_specs, check_vma=False
    )
```

```python
import functools
import jax
import jax.numpy as jnp
from jax import lax
from jax.experimental import pallas as pl
from jax.experimental.pallas import tpu as pltpu
from jax.sharding import PartitionSpec as P

MICRO = 8
CHUNK = 256
PART = 512
APART = 2
EARLY = 2
PIECES = 10
SHIFTED = 1
WINDOW = 384

branch_scale = 0.5
norm_eps = 1e-05
beta_one = 0.9
beta_two = 0.95
adam_eps = 1e-08
learn_rate = 0.01
step_count = 4.0
tanh_coef = 0.7978845608028654
cubic_coef = 0.044715


def chain_kernel(
    sections,
    replicas,
    inputs_ref,
    cotangent_ref,
    shard_ref,
    moment_one_ref,
    moment_two_ref,
    update_ref,
    shadow_weight_ref,
    shadow_ref,
    weight,
    flipped,
    arrived,
    outputs,
    grads_in,
    grads_out,
    pre_acts,
    slopes,
    scales,
    normed_all,
    units,
    units_flipped,
    gathered,
    moment_one,
    moment_two,
    fresh,
    stage,
    sums,
    load_sem,
    ahead_send,
    ahead_recv,
    back_send,
    back_recv,
    shadow_send,
    shadow_recv,
    weight_send,
    weight_recv,
    grad_send,
    grad_recv,
    unit_send,
    unit_recv,
    fresh_send,
    fresh_recv,
    part_send,
    part_recv,
    passed,
):
    micro, rows, width = arrived.shape
    shard = width // replicas
    piece = shard // PIECES
    ring = replicas // 2
    tokens = micro * rows
    blocks = width // CHUNK
    pairs = micro // 2
    me = lax.axis_index("section")
    mine = lax.axis_index("dp")
    after = lax.rem(me + 1, sections)
    before = lax.rem(me + sections - 1, sections)
    line, side = mine // 2, lax.rem(mine, 2)

    def peer(step, across=False):
        return lax.rem(line + step + ring, ring) * 2 + (1 - side if across else side)

    right, left, facing, far = peer(1), peer(-1), peer(0, True), peer(2)

    loads = [
        pltpu.make_async_copy(
            shard_ref,
            weight.at[pl.ds(pl.multiple_of(mine * shard, 16), shard)],
            load_sem.at[0],
        ),
        pltpu.make_async_copy(moment_one_ref, moment_one, load_sem.at[1]),
        pltpu.make_async_copy(moment_two_ref, moment_two, load_sem.at[2]),
    ]
    loads[0].start()
    barrier = pltpu.get_barrier_semaphore()
    later = lax.rem(me + APART, sections)
    earlier = lax.rem(me + sections - APART, sections)
    for other in (before, after, earlier, later):
        pl.semaphore_signal(barrier, inc=1, device_id={"section": other})
    for step in range(1, replicas):
        pl.semaphore_signal(barrier, inc=1, device_id={"dp": lax.rem(mine + step, replicas)})
    pl.semaphore_wait(barrier, replicas + 3)

    def spread_over(place, own, sends, recvs, crosses, shifted):
        def move(lane, owner, i, to, source=None):
            return pltpu.make_async_remote_copy(
                src_ref=place(owner, i) if source is None else source,
                dst_ref=place(owner, i),
                send_sem=sends.at[lane, i],
                recv_sem=recvs.at[owner, i],
                device_id={"dp": to},
            )

        def landed(owner, i):
            move(0, owner, i, mine).wait_recv()

        def spread_line(i):
            move(1, mine, i, right, own(i)).start()
            move(2, mine, i, left, own(i)).start()

        def spread_face(i):
            move(0, mine, i, facing, own(i)).start()

        def pass_on(i):
            turn = 2 * lax.rem(i, 2) - 1
            landed(peer(turn), i)
            move(3, peer(turn), i, peer(-turn)).start()

        def relay(i):
            turn = 2 * lax.rem(i, 2) - 1
            landed(facing, i)

            @pl.when(i >= shifted)
            def _():
                move(4, facing, i, right).start()
                move(5, facing, i, left).start()

            @pl.when(i < shifted)
            def _():
                landed(peer(-turn), i)
                move(4, peer(turn), i, facing).start()
                move(5, peer(-turn), i, facing).start()

        def cross(i):
            turn = 2 * lax.rem(i, 2) - 1

            @pl.when(crosses(i))
            def _():
                landed(far, i)
                move(6, far, i, facing).start()

            @pl.when(jnp.logical_not(crosses(i)))
            def _():
                landed(peer(turn, True), i)
                move(6, peer(turn, True), i, peer(-turn)).start()

        def finish(i):
            turn = 2 * lax.rem(i, 2) - 1

            @pl.when(i >= shifted)
            def _():
                landed(peer(-turn), i)

            landed(peer(-turn, True), i)
            landed(peer(2, True), i)

            @pl.when(crosses(i))
            def _():
                landed(peer(turn, True), i)

            @pl.when(jnp.logical_not(crosses(i)))
            def _():
                landed(far, i)

        def sent(i):
            for lane in range(7):
                move(lane, mine, i, mine).wait_send()

        return spread_line, spread_face, pass_on, relay, cross, finish, sent

    def each(count, *steps, first=0):
        for step in steps:

            def one(i, carry, step=step):
                step(i)
                return carry

            lax.fori_loop(first, first + count, one, 0)

    def weight_place(owner, i):
        return weight.at[pl.ds(pl.multiple_of(owner * shard + i * piece, 16), piece)]

    weight_spread = spread_over(
        weight_place,
        lambda i: shard_ref.at[pl.ds(pl.multiple_of(i * piece, 16), piece)],
        weight_send,
        weight_recv,
        lambda i: i >= 0,
        SHIFTED,
    )

    def grad_place(owner, i):
        pair = pl.ds(2 * lax.rem(i, pairs), 2)
        half = pl.ds(pl.multiple_of((i // pairs) * (width // 2), 128), width // 2)
        return gathered.at[owner, pair, :, half]

    (
        grad_line,
        grad_face,
        grad_pass,
        grad_relay,
        grad_cross,
        grad_finish,
        grad_sent,
    ) = spread_over(
        grad_place,
        lambda i: grad_place(mine, i),
        grad_send,
        grad_recv,
        lambda i: (me < 2) | (lax.rem(i // 2, 2) == 0),
        0,
    )

    def ahead(i):
        return pltpu.make_async_remote_copy(
            src_ref=outputs.at[i],
            dst_ref=arrived.at[i],
            send_sem=ahead_send.at[i],
            recv_sem=ahead_recv.at[i],
            device_id={"section": after},
        )

    def ahead_part(i, k):
        part = pl.ds(k * PART, PART)
        return pltpu.make_async_remote_copy(
            src_ref=outputs.at[i, :, part],
            dst_ref=arrived.at[i, :, part],
            send_sem=part_send.at[0, i, k],
            recv_sem=part_recv.at[0, i, k],
            device_id={"section": after},
        )

    def back(i):
        return pltpu.make_async_remote_copy(
            src_ref=grads_out.at[i],
            dst_ref=grads_in.at[i],
            send_sem=back_send.at[i],
            recv_sem=back_recv.at[i],
            device_id={"section": before},
        )

    def back_part(i, k):
        part = pl.ds(k * PART, PART)
        return pltpu.make_async_remote_copy(
            src_ref=grads_out.at[i, :, part],
            dst_ref=grads_in.at[i, :, part],
            send_sem=part_send.at[1, i, k],
            recv_sem=part_recv.at[1, i, k],
            device_id={"section": before},
        )

    def shadow(i):
        return pltpu.make_async_remote_copy(
            src_ref=outputs.at[i],
            dst_ref=shadow_ref.at[i],
            send_sem=shadow_send.at[i],
            recv_sem=shadow_recv.at[i],
            device_id={"section": before},
        )

    def window(owner):
        start = (owner // 2) * (2 * shard) + lax.rem(owner, 2) * (2 * shard - WINDOW)
        return normed_all.at[:, :, pl.ds(pl.multiple_of(start, 128), WINDOW)]

    def unit(step):
        to = lax.rem(mine + step, replicas)
        return pltpu.make_async_remote_copy(
            src_ref=window(to),
            dst_ref=units.at[mine],
            send_sem=unit_send.at[step],
            recv_sem=unit_recv.at[step],
            device_id={"dp": to},
        )

    def columns(k):
        return pl.ds(pl.multiple_of(k * CHUNK, CHUNK), CHUNK)

    def fresh_move(k):
        return pltpu.make_async_remote_copy(
            src_ref=fresh.at[:, columns(k)],
            dst_ref=shadow_weight_ref.at[:, columns(k)],
            send_sem=fresh_send.at[k],
            recv_sem=fresh_recv.at[k],
            device_id={"section": before},
        )

    def flip(k):
        row, column = columns(k // blocks), columns(lax.rem(k, blocks))
        flipped[column, row] = weight[row, column].T

    *weight_steps, weight_sent = weight_spread
    each(PIECES, *weight_steps)
    loads[0].wait()
    loads[1].start()
    loads[2].start()

    @pl.when(me == 0)
    def _():
        arrived[...] = inputs_ref[...]

    @pl.when(me == sections - 1)
    def _():
        grads_in[...] = cotangent_ref[...]

    @pl.when(me >= sections // 2)
    def _():
        each(blocks * blocks, flip)

    def keep(i, at, v, t):
        part = pl.ds(at, PART)
        pre_acts[i, :, part] = v
        slope = 0.5 * (1.0 + t) + 0.5 * v * (1.0 - t * t) * tanh_coef * (
            1.0 + 3.0 * cubic_coef * v * v
        )
        slopes[i, :, part] = branch_scale * slope

    def finish_output(i, at, v):
        part = pl.ds(at, PART)
        t = jnp.tanh(tanh_coef * (v + cubic_coef * v * v * v))
        out = arrived[i, :, part].astype(jnp.float32) + branch_scale * (0.5 * v * (1.0 + t))
        outputs[i, :, part] = out.astype(jnp.bfloat16)
        return t

    def rms_scale(squares):
        return lax.rsqrt(squares * (1.0 / width) + norm_eps)

    def lanes(values):
        total = values[:, :128]
        for at in range(128, values.shape[1], 128):
            total += values[:, at : at + 128]
        return total

    def row_total(partial):
        return jnp.sum(partial, axis=-1, keepdims=True)

    def forward_spread(last, i):
        ahead(i).wait_recv()
        raw = arrived[i]

        def product(at):
            return jnp.dot(raw, weight[:, pl.ds(at, PART)], preferred_element_type=jnp.float32)

        following = product(0)
        current = raw.astype(jnp.float32)
        scale = rms_scale(row_total(lanes(current * current)))
        scales[i] = jnp.broadcast_to(scale, (rows, 128))
        for at in range(0, width, PART):
            v = following * scale
            if at + PART < width:
                following = product(at + PART)
            t = finish_output(i, at, v)
            if at + PART < width:
                keep(i, at, v, t)
            if not last:
                ahead_part(i, at // PART).start()
        keep(i, at, v, t)
        normed_all[i] = (arrived[i].astype(jnp.float32) * scale).astype(jnp.bfloat16)

    def forward_collect(first, i):
        squares = jnp.zeros((rows, 128), jnp.float32)
        for at in range(0, width - PART, PART):
            part = pl.ds(at, PART)
            if not first:
                ahead_part(i, at // PART).wait_recv()
            raw = arrived[i, :, part]
            current = raw.astype(jnp.float32)
            squares += lanes(current * current)
            product = jnp.dot(raw, weight[part, :], preferred_element_type=jnp.float32)
            if at == 0:
                sums[...] = product
            else:
                sums[...] += product
        end = pl.ds(width - PART, PART)
        if not first:
            ahead_part(i, width // PART - 1).wait_recv()
        raw = arrived[i, :, end]

        def product(at):
            part = pl.ds(at, PART)
            return sums[:, part] + jnp.dot(
                raw, weight[end, part], preferred_element_type=jnp.float32
            )

        current = raw.astype(jnp.float32)
        scale = rms_scale(row_total(squares + lanes(current * current)))
        values = []
        following = product(0)
        for at in range(0, width, PART):
            v = following * scale
            if at + PART < width:
                following = product(at + PART)
            values.append((at, v, finish_output(i, at, v)))
        ahead(i).start()
        for at, v, t in values:
            keep(i, at, v, t)
        scales[i] = jnp.broadcast_to(scale, (rows, 128))
        normed_all[i] = (arrived[i].astype(jnp.float32) * scale).astype(jnp.bfloat16)

    odd = lax.rem(me, 2)

    @pl.when((odd == 1) & (me < sections - 1))
    def _():
        each(micro, functools.partial(forward_spread, False))

    @pl.when(me == sections - 1)
    def _():
        each(micro, functools.partial(forward_spread, True))

    @pl.when((odd == 0) & (me > 0))
    def _():
        each(micro, functools.partial(forward_collect, False))

    @pl.when(me == 0)
    def _():
        each(micro, functools.partial(forward_collect, True))

    def send_units():
        for step in range(1, replicas):
            unit(step).start()
        units[mine] = window(mine)[...]

    def flip_units():
        for step in range(1, replicas):
            unit(step).wait_recv()

        def one(k):
            block = units[k].reshape(tokens, WINDOW)
            units_flipped[:, pl.ds(pl.multiple_of(k * tokens, tokens), tokens)] = block.T

        each(replicas, one)

    @pl.when(me < sections // 2)
    def _():
        each(micro, lambda i: shadow(i).start())
        each(blocks * blocks, flip)
        send_units()
        flip_units()

    def finish_grad(i, at, g, scale, pull):
        part = pl.ds(at, PART)
        a = arrived[i, :, part].astype(jnp.float32)
        total = grads_in[i, :, part].astype(jnp.float32) + scale * g - pull * a
        grads_out[i, :, part] = total.astype(jnp.bfloat16)

    def push_grads(i):
        @pl.when(lax.rem(i, 2) == 1)
        def _():
            for half in range(2):
                grad_line(half * pairs + i // 2)

                @pl.when(me < EARLY)
                def _(half=half):
                    grad_face(half * pairs + i // 2)

    def backward_spread(i):
        back(i).wait_recv()
        grad_pre = (grads_in[i].astype(jnp.float32) * slopes[i]).astype(jnp.bfloat16)
        gathered[mine, i] = grad_pre

        @pl.when(me > 0)
        def _():
            overlap = jnp.sum(
                grad_pre.astype(jnp.float32) * pre_acts[i], axis=-1, keepdims=True
            ) * (1.0 / width)
            scale = scales[i][:, :1]
            pull = scale * scale * overlap

            def product(at):
                return jnp.dot(
                    grad_pre, flipped[:, pl.ds(at, PART)], preferred_element_type=jnp.float32
                )

            following = product(0)
            for at in range(0, width, PART):
                g = following
                if at + PART < width:
                    following = product(at + PART)
                finish_grad(i, at, g, scale, pull)
                back_part(i, at // PART).start()
        push_grads(i)

    def backward_collect(first, i):
        overlap = jnp.zeros((rows, 128), jnp.float32)

        def grad_part(at):
            part = pl.ds(at, PART)
            if not first:
                back_part(i, at // PART).wait_recv()
            grad_pre = (grads_in[i, :, part].astype(jnp.float32) * slopes[i, :, part]).astype(
                jnp.bfloat16
            )
            gathered[mine, i, :, part] = grad_pre
            return grad_pre, lanes(grad_pre.astype(jnp.float32) * pre_acts[i, :, part])

        for at in range(0, width - PART, PART):
            grad_pre, extra = grad_part(at)
            overlap += extra
            product = jnp.dot(
                grad_pre, flipped[pl.ds(at, PART), :], preferred_element_type=jnp.float32
            )
            if at == 0:
                sums[...] = product
            else:
                sums[...] += product
        grad_pre, extra = grad_part(width - PART)
        end = pl.ds(width - PART, PART)

        def finish_product(at):
            part = pl.ds(at, PART)
            return sums[:, part] + jnp.dot(
                grad_pre, flipped[end, part], preferred_element_type=jnp.float32
            )

        following = finish_product(0)
        scale = scales[i][:, :1]
        pull = scale * scale * row_total(overlap + extra) * (1.0 / width)
        for at in range(0, width, PART):
            g = following
            if at + PART < width:
                following = finish_product(at + PART)
            finish_grad(i, at, g, scale, pull)
        back(i).start()
        push_grads(i)

    @pl.when(odd == 0)
    def _():
        each(micro, backward_spread)

    @pl.when((odd == 1) & (me < sections - 1))
    def _():
        each(micro, functools.partial(backward_collect, False))

    @pl.when(me == sections - 1)
    def _():
        each(micro, functools.partial(backward_collect, True))

    @pl.when((me > 0) & (me < sections - APART))
    def _():
        pl.semaphore_signal(passed, inc=1, device_id={"section": later})

    @pl.when(me > APART)
    def _():
        pl.semaphore_wait(passed, 1)

    @pl.when(me >= EARLY)
    def _():
        each(micro, grad_face)

    each(micro, grad_pass, grad_relay, grad_cross)

    @pl.when(me >= sections // 2)
    def _():
        each(micro, lambda i: shadow(i).start())
        send_units()
        flip_units()

    loads[1].wait()
    loads[2].wait()
    skip = lax.rem(mine, 2) * (WINDOW - shard)
    own_rows = mine * shard
    strip = shard // 5

    def step_weights(k):
        part = columns(k)
        grads = gathered[:, :, :, part].reshape(replicas * tokens, CHUNK)
        stage[...] = jnp.dot(units_flipped[...], grads, preferred_element_type=jnp.float32) * (
            1.0 / (replicas * tokens)
        )

        def adam(j):
            here = pl.ds(pl.multiple_of(j * strip, strip), strip)
            gradient = stage[pl.ds(pl.multiple_of(skip + j * strip, 16), strip), :]
            one = beta_one * moment_one[here, part] + (1.0 - beta_one) * gradient
            two = beta_two * moment_two[here, part] + (1.0 - beta_two) * gradient * gradient
            corrected_one = one * (1.0 / (1.0 - beta_one**step_count))
            corrected_two = two * (1.0 / (1.0 - beta_two**step_count))
            direction = corrected_one / (jnp.sqrt(corrected_two) + adam_eps)
            old = weight[pl.ds(pl.multiple_of(own_rows + j * strip, 16), strip), part]
            update_ref[here, part] = direction.astype(jnp.bfloat16)
            fresh[here, part] = (old.astype(jnp.float32) - learn_rate * direction).astype(
                jnp.bfloat16
            )

        each(5, adam)
        fresh_move(k).start()

    for half in range(2):
        each(pairs, grad_finish, first=half * pairs)
        each(blocks // 2, step_weights, first=half * (blocks // 2))

    def settle(i):
        @pl.when(odd == 0)
        def _():
            ahead(i).wait_send()

        @pl.when(odd == 1)
        def _():
            back(i).wait_send()

        for k in range(width // PART):

            @pl.when((odd == 1) & (me < sections - 1))
            def _(k=k):
                ahead_part(i, k).wait_send()

            @pl.when((odd == 0) & (me > 0))
            def _(k=k):
                back_part(i, k).wait_send()

        shadow(i).wait_send()
        shadow(i).wait_recv()

    def settle_fresh(k):
        fresh_move(k).wait_send()
        fresh_move(k).wait_recv()

    each(PIECES, weight_sent)
    each(micro, settle, grad_sent)
    for step in range(1, replicas):
        unit(step).wait_send()
    each(blocks, settle_fresh)


def on_device(inputs, cotangent, weights, adam_m, adam_v):
    sections = lax.axis_size("section")
    replicas = lax.axis_size("dp")
    tokens, width = inputs.shape
    shard = width // replicas
    rows = tokens // MICRO
    block = (MICRO, rows, width)
    low = jnp.bfloat16
    wide = jnp.float32
    in_vmem = pl.BlockSpec(memory_space=pltpu.VMEM)
    anywhere = pl.BlockSpec(memory_space=pl.ANY)
    dma = pltpu.SemaphoreType.DMA
    update, shadow_weight, shadow_output = pl.pallas_call(
        functools.partial(chain_kernel, sections, replicas),
        out_shape=(
            jax.ShapeDtypeStruct((shard, width), low),
            jax.ShapeDtypeStruct((shard, width), low),
            jax.ShapeDtypeStruct(block, low),
        ),
        in_specs=[in_vmem, in_vmem, anywhere, anywhere, anywhere],
        out_specs=(in_vmem, anywhere, anywhere),
        scratch_shapes=[
            pltpu.VMEM((width, width), low),
            pltpu.VMEM((width, width), low),
            pltpu.VMEM(block, low),
            pltpu.VMEM(block, low),
            pltpu.VMEM(block, low),
            pltpu.VMEM(block, low),
            pltpu.VMEM(block, wide),
            pltpu.VMEM(block, wide),
            pltpu.VMEM((MICRO, rows, 128), wide),
            pltpu.VMEM(block, low),
            pltpu.VMEM((replicas, MICRO, rows, WINDOW), low),
            pltpu.VMEM((WINDOW, replicas * tokens), low),
            pltpu.VMEM((replicas,) + block, low),
            pltpu.VMEM((shard, width), wide),
            pltpu.VMEM((shard, width), wide),
            pltpu.VMEM((shard, width), low),
            pltpu.VMEM((WINDOW, CHUNK), wide),
            pltpu.VMEM((rows, width), wide),
            dma((3,)),
        ]
        + [dma((MICRO,))] * 6
        + [
            dma((7, PIECES)),
            dma((replicas, PIECES)),
            dma((7, MICRO)),
            dma((replicas, MICRO)),
            dma((replicas,)),
            dma((replicas,)),
            dma((width // CHUNK,)),
            dma((width // CHUNK,)),
            dma((2, MICRO, width // PART)),
            dma((2, MICRO, width // PART)),
            pltpu.SemaphoreType.REGULAR,
        ],
        compiler_params=pltpu.CompilerParams(
            collective_id=0, has_side_effects=True, vmem_limit_bytes=60 * 2**20
        ),
        cost_estimate=pl.CostEstimate(
            flops=6 * tokens * width * width,
            bytes_accessed=16 * shard * width,
            transcendentals=tokens * width,
        ),
    )(
        inputs.reshape(block),
        cotangent.reshape(block),
        weights[0],
        adam_m[0],
        adam_v[0],
    )
    return (update[None], shadow_weight[None], shadow_output.reshape(1, tokens, width))


def solution(mesh):
    in_specs = (
        P("dp", None),
        P("dp", None),
        P("section", "dp", None),
        P("section", "dp", None),
        P("section", "dp", None),
    )
    out_specs = (P("section", "dp", None), P("section", "dp", None), P("section", "dp", None))
    return jax.shard_map(
        on_device, mesh=mesh, in_specs=in_specs, out_specs=out_specs, check_vma=False
    )
```
